32 devices in a mesh: groups: 2 (over y), wide: 4 (over z), narrow: 2 (over x), inner: 2 (over core).
Axes of the slice: x: 2, y: 2, z: 4, core: 2. Of those that a mesh axis runs over, the one named last changes fastest.
Arguments:
- land_cover: int32 [192, 512], P(('groups', 'wide'), ('narrow', 'inner')), parts along dimension 0, may hold values from 0 to 15
- prune_mask: int32 [2, 192, 512], P(None, ('groups', 'wide'), ('narrow', 'inner')), parts along dimension 1, may hold values 0 or 1
- class_resistance: float32 [16], replicated, may hold values from 1 to 100
- source_cells: int32 [256], P('groups'), parts along dimension 0, may hold values from 0 to 49151
- ground_cells: int32 [256], P('groups'), parts along dimension 0, may hold values from 0 to 49151
- warm_start: float32 [128, 192, 512], P(None, ('groups', 'wide'), ('narrow', 'inner')), parts along dimension 1, may hold values from -24 to 24
Outputs:
- potentials: float32 [128, 192, 512], P(None, ('groups', 'wide'), ('narrow', 'inner')), parts along dimension 1
- residual: float32 [128, 192, 512], P(None, ('groups', 'wide'), ('narrow', 'inner')), parts along dimension 1
The draws below stay inside these ranges and needn't reach their ends.
There are 2 independent parts, one for each index of `groups`. The reference program is written for one: setup_inputs(seed, part) draws one part's arguments, and reference() takes and returns one part's arrays. A program takes and returns all parts, laid end to end along the dimension named above; an argument that names none is the same for every part. Nothing has to cross between parts.
All inputs are finite; a program needn't handle non-finite values. No bound on the sum of `prune_mask` on one device may be relied on, other than what follows from the above.
Results may differ from the reference program's by a relative error of at most 0.0025.
Values sent between devices are 32-bit elements; how exact they have to be, the bound alone decides.
A program may use at most 64 MiB of HBM per device.

```python
import math
import jax
import jax.numpy as jnp
from jax import lax

PAIRS = 128
NCLASS = 16
ITERS = 2
NR = 96
NC = 512


def draw_warm_start(key, part):
    key = jax.random.fold_in(key, 1)
    first = jax.random.fold_in(key, 0)
    rows = jnp.arange(NR, dtype=jnp.float32)
    rise = (1.0 + 2.0 * rows / max(NR - 1, 1))[None, :, None]
    values = jax.random.normal(first, (PAIRS, NR, NC), jnp.float32) * rise
    return jnp.clip(values, -24.0, 24.0)


def place_ends(drawn, rng, smallest, high):
    place = [jax.random.randint(jax.random.fold_in(rng, axis), (), 0, length) for axis, length in enumerate(drawn.shape)]
    widest = drawn.shape.index(max(drawn.shape))
    neighbour = place[:widest] + [(place[widest] + 1) % drawn.shape[widest]] + place[widest + 1:]
    return drawn.at[tuple(place)].set(smallest).at[tuple(neighbour)].set(high)


def setup_inputs(seed: int = 0, part: int = 0) -> dict:
    key_of = jax.random.split(jax.random.key(seed), 7)
    part_splits = jax.random.split(jax.random.fold_in(key_of[6], part), 7)
    land_cover = place_ends(jax.random.randint(part_splits[0], (NR, NC), 0, NCLASS), jax.random.fold_in(part_splits[0], 1), 0, NCLASS - 1).astype(jnp.int32)
    prune_mask = place_ends((jax.random.randint(part_splits[1], (2, NR, NC), 0, 4) < 1).astype(jnp.int32), jax.random.fold_in(part_splits[1], 1), 0, 1)
    class_resistance = jnp.clip(jnp.exp(jax.random.uniform(key_of[2], (NCLASS,), jnp.float32, math.log(1.0), math.log(100.0))), 1.0, 100.0)
    source_cells = place_ends(jax.random.randint(part_splits[3], (PAIRS,), 0, NR * NC), jax.random.fold_in(part_splits[3], 1), 0, (NR * NC) - 1).astype(jnp.int32)
    ground_cells = place_ends(jax.random.randint(part_splits[4], (PAIRS,), 0, NR * NC), jax.random.fold_in(part_splits[4], 1), 0, (NR * NC) - 1).astype(jnp.int32)
    warm_start = draw_warm_start(jax.random.fold_in(jax.random.fold_in(key_of[6], part), 71), part)
    return dict(land_cover=land_cover, prune_mask=prune_mask, class_resistance=class_resistance, source_cells=source_cells, ground_cells=ground_cells, warm_start=warm_start)


LEAK = 0.1

def resist(cover, table):
    classes = jnp.arange(table.shape[0], dtype=jnp.int32)
    hit = cover[None] == classes[:, None, None]
    return jnp.sum(jnp.where(hit, table[:, None, None], jnp.float32(0.0)), 0)

def conductances(cover, prune, table):
    res = resist(cover, table)
    rows, cols = res.shape
    right = jnp.pad(res[:, 1:], ((0, 0), (0, 1)), constant_values=1.0)
    below = jnp.pad(res[1:, :], ((0, 1), (0, 0)), constant_values=1.0)
    col_ids = lax.broadcasted_iota(jnp.int32, (rows, cols), 1)
    row_ids = lax.broadcasted_iota(jnp.int32, (rows, cols), 0)
    keep_right = (1 - prune[0]).astype(jnp.float32) * (col_ids < cols - 1).astype(jnp.float32)
    keep_down = (1 - prune[1]).astype(jnp.float32) * (row_ids < rows - 1).astype(jnp.float32)
    return (keep_right * 2.0 / (res + right), keep_down * 2.0 / (res + below))

def operate(field, right_cond, down_cond):
    padded = jnp.pad(field, ((0, 0), (1, 1), (1, 1)))
    center = padded[:, 1:-1, 1:-1]
    right_left = jnp.pad(right_cond, ((0, 0), (1, 0)))[:, :-1]
    down_up = jnp.pad(down_cond, ((1, 0), (0, 0)))[:-1, :]
    total = LEAK * center
    total = total + right_cond * (center - padded[:, 1:-1, 2:])
    total = total + right_left * (center - padded[:, 1:-1, :-2])
    total = total + down_cond * (center - padded[:, 2:, 1:-1])
    total = total + down_up * (center - padded[:, :-2, 1:-1])
    return total

def gram(left, right):
    count = left.shape[0]
    return jnp.dot(left.reshape(count, -1), right.reshape(count, -1).T, precision=lax.Precision.HIGHEST)

def symm(matrix):
    return 0.5 * (matrix + matrix.T)

def spd_solve(matrix, rhs):
    factor = jnp.linalg.cholesky(matrix)
    return jax.scipy.linalg.cho_solve((factor, True), rhs)

def combine(coeffs, field):
    count = field.shape[0]
    out = jnp.dot(coeffs.T, field.reshape(count, -1), precision=lax.Precision.HIGHEST)
    return out.reshape(field.shape)

def reference(land_cover, prune_mask, class_resistance, source_cells, ground_cells, warm_start):
    right_cond, down_cond = conductances(land_cover, prune_mask, class_resistance)
    rows, cols = land_cover.shape
    flat = lax.broadcasted_iota(jnp.int32, (rows, cols), 0) * cols + lax.broadcasted_iota(jnp.int32, (rows, cols), 1)
    currents = (flat[None] == source_cells[:, None, None]).astype(jnp.float32) - (flat[None] == ground_cells[:, None, None]).astype(jnp.float32)
    potentials = warm_start
    residual = currents - operate(potentials, right_cond, down_cond)
    direction = residual
    norm_now = symm(gram(residual, residual))
    for step in range(ITERS):
        image = operate(direction, right_cond, down_cond)
        alpha = spd_solve(symm(gram(direction, image)), norm_now)
        potentials = potentials + combine(alpha, direction)
        residual = residual - combine(alpha, image)
        if step + 1 < ITERS:
            norm_next = symm(gram(residual, residual))
            beta = spd_solve(norm_now, norm_next)
            direction = residual + combine(beta, direction)
            norm_now = norm_next
    return (potentials, residual)
```

```python
import functools
import jax
import jax.numpy as jnp
from jax import lax
from jax.experimental import pallas as pl
from jax.experimental.pallas import tpu as pltpu
from jax.sharding import PartitionSpec as P

LEAK = 0.1
MESH = pl.DeviceIdType.MESH
F32 = jnp.float32
GROUP = 16
BLOCK = 16
NT = (((1,), (1,)), ((), ()))
NN = (((1,), (0,)), ((), ()))


def split(x):
    hi = x.astype(jnp.bfloat16)
    return hi, (x - hi.astype(F32)).astype(jnp.bfloat16)


def dot3(a, b, dims):
    (ah, al), (bh, bl) = a, b
    mm = functools.partial(lax.dot_general, dimension_numbers=dims, preferred_element_type=F32)
    return mm(ah, bh) + (mm(ah, bl) + mm(al, bh))


def stages_of(count):
    out, stride = [], 1
    while count > 1:
        g = min(GROUP, count)
        assert count % g == 0
        out.append((g, stride))
        stride *= g
        count //= g
    return out


def krylov_kernel(sizes, pieces, cover_ref, prune_ref, table_ref, src_ref, gnd_ref, x_ref,
                  r0_ref, w1_ref, w2_ref, gram_ref,
                  fx, f0, f1, packs, lefts, rights, edge, edge_up, edge_down, side, side_left, side_right,
                  cond, sg, hsend, hrecv, isend, irecv, gsend, grecv, *bufs):
    wide_n, narrow_n, inner_n = sizes
    pairs = fx.shape[1]
    rows, cols = cover_ref.shape
    cells_n = narrow_n * inner_n
    stages = stages_of(wide_n * cells_n)
    w = lax.axis_index("wide")
    c = lax.axis_index("narrow") * inner_n + lax.axis_index("inner")
    rank = w * cells_n + c

    def dev(rk):
        return {"wide": rk // cells_n, "narrow": (rk % cells_n) // inner_n, "inner": rk % inner_n}

    has_up, has_down = w > 0, w < wide_n - 1
    has_left, has_right = c > 0, c < cells_n - 1
    sides = ((has_up, rank - cells_n), (has_down, rank + cells_n), (has_left, rank - 1), (has_right, rank + 1))

    def peer(stage, o):
        g, stride = stages[stage]
        digit = (rank // stride) % g
        other = (digit + o) % g
        return other, rank + (other - digit) * stride

    barrier = pltpu.get_barrier_semaphore()
    expect = 0
    for s, (g, _) in enumerate(stages):
        for o in range(1, g):
            pl.semaphore_signal(barrier, inc=1, device_id=dev(peer(s, o)[1]), device_id_type=MESH)
            expect += 1
    near = 0
    if len(stages) > 1:
        for has, rk in sides:
            near = near + has.astype(jnp.int32)

            @pl.when(has)
            def _(rk=rk):
                pl.semaphore_signal(barrier, inc=1, device_id=dev(rk), device_id_type=MESH)

    lane = lax.broadcasted_iota(jnp.int32, (pairs, cols), 1)
    half = pairs // 2
    lane_h = lax.broadcasted_iota(jnp.int32, (half, cols), 1)

    cover = cover_ref[...]
    res = jnp.zeros((rows, cols), F32)
    for k in range(table_ref.shape[0]):
        res = jnp.where(cover == k, table_ref[k], res)
    keep_r = (1 - prune_ref[0]).astype(F32)
    keep_d = (1 - prune_ref[1]).astype(F32)
    side[0] = res
    side[1] = keep_r
    edge[...] = jnp.concatenate([res[:1], res[rows - 1:], keep_d[rows - 1:], res[: 5]], 0)

    zero_row = jnp.zeros((pairs, cols), F32)
    for has, bufs0 in ((has_up, tuple(f.at[0] for f in (fx, f0, f1))),
                       (has_down, tuple(f.at[rows + 1] for f in (fx, f0, f1))),
                       (has_left, tuple(lefts.at[e] for e in range(3))),
                       (has_right, tuple(rights.at[e] for e in range(3)))):
        @pl.when(jnp.logical_not(has))
        def _(bufs0=bufs0):
            for b in bufs0:
                b[...] = zero_row

    for has, ref in ((has_up, edge_up), (has_down, edge_down), (has_left, side_left), (has_right, side_right)):
        @pl.when(jnp.logical_not(has))
        def _(ref=ref):
            ref[...] = jnp.ones(ref.shape, F32)

    packs[0] = zero_row

    def load_row(r, carry):
        v = x_ref[pl.ds(r, pairs, stride=rows), :]
        fx[r + 1] = v
        rolled = pltpu.roll(v, 2 * r, 1)
        packs[0] = jnp.where((lane == 2 * r) | (lane == (2 * r + cols - 1) % cols), rolled, packs[0])
        return carry

    lax.fori_loop(0, rows, load_row, 0)
    pl.semaphore_wait(barrier, expect + near)

    def halo(e):
        field = (fx, f0, f1)[e]
        return (
            (field.at[1], field.at[rows + 1], 0),
            (field.at[rows], field.at[0], 1),
            (packs.at[e], rights.at[e], 2),
            (packs.at[e], lefts.at[e], 3),
        )

    def copies(items, ssem, rsem):
        out = []
        for (src, dst, k), (has, rk) in zip(items, sides):
            out.append((has, pltpu.make_async_remote_copy(
                src_ref=src, dst_ref=dst, send_sem=ssem.at[k], recv_sem=rsem.at[k],
                device_id=dev(rk), device_id_type=MESH)))
        return out

    def start(cs):
        for has, cp in cs:
            @pl.when(has)
            def _(cp=cp):
                cp.start()

    def wait(cs):
        order = (1, 0, 3, 2)
        for k, (has, cp) in enumerate(cs):
            @pl.when(has)
            def _(cp=cp):
                cp.wait_send()

            @pl.when(cs[order[k]][0])
            def _(cp=cp):
                cp.wait_recv()

    info = copies(((edge, edge_down, 0), (edge, edge_up, 1), (side, side_right, 2), (side, side_left, 3)), isend, irecv)
    start(info)
    ex = [copies(halo(e), hsend.at[e], hrecv.at[e]) for e in range(3)]
    start(ex[0])

    src_t = jnp.broadcast_to(src_ref[...].astype(F32), (cols, pairs)).T
    gnd_t = jnp.broadcast_to(gnd_ref[...].astype(F32), (cols, pairs)).T
    sg[0] = src_t
    sg[1] = gnd_t

    wait(info)
    lane_r = lax.broadcasted_iota(jnp.int32, (rows, cols), 1)
    row_r = lax.broadcasted_iota(jnp.int32, (rows, cols), 0)
    right_res = jnp.where(lane_r == cols - 1, pltpu.roll(side_right[0], cols - 1, 1), pltpu.roll(res, cols - 1, 1))
    left_res = jnp.where(lane_r == 0, pltpu.roll(side_left[0], 1, 1), pltpu.roll(res, 1, 1))
    left_keep = jnp.where(lane_r == 0, pltpu.roll(side_left[1], 1, 1), pltpu.roll(keep_r, 1, 1))
    down_res = jnp.where(row_r == rows - 1, edge_down[0:1, :], pltpu.roll(res, rows - 1, 0))
    up_res = jnp.where(row_r == 0, edge_up[1:2, :], pltpu.roll(res, 1, 0))
    up_keep = jnp.where(row_r == 0, edge_up[2:3, :], pltpu.roll(keep_d, 1, 0))
    at_right = (lane_r == cols - 1) & jnp.logical_not(has_right)
    at_left = (lane_r == 0) & jnp.logical_not(has_left)
    at_down = (row_r == rows - 1) & jnp.logical_not(has_down)
    at_up = (row_r == 0) & jnp.logical_not(has_up)
    cond[0] = jnp.where(at_right, 0.0, keep_r * 2.0 / (res + right_res))
    cond[1] = jnp.where(at_left, 0.0, left_keep * 2.0 / (res + left_res))
    cond[2] = jnp.where(at_down, 0.0, keep_d * 2.0 / (res + down_res))
    cond[3] = jnp.where(at_up, 0.0, up_keep * 2.0 / (res + up_res))

    def stencil(e, finish):
        field = (fx, f0, f1)[e]
        even = (lane % 2) == 0
        lefts[e] = jnp.where(even, rights[e], pltpu.roll(lefts[e], 2, 1))
        if e < 2:
            packs[e + 1] = zero_row

        def body(r, carry):
            cr, cl, cd, cu = (cond[k, pl.ds(r, 1), :] for k in range(4))
            for h in range(2):
                hs = pl.ds(h * half, half)
                v = field[r + 1, hs, :]
                edges = pltpu.roll(lefts[e, hs, :], (2 * cols - 2 * r - 1) % cols, 1)
                xr = jnp.where(lane_h == cols - 1, edges, pltpu.roll(v, cols - 1, 1))
                xl = jnp.where(lane_h == 0, edges, pltpu.roll(v, 1, 1))
                lap = cr * (v - xr) + cl * (v - xl) + cd * (v - field[r + 2, hs, :]) + cu * (v - field[r, hs, :])
                out = finish(r, hs, v, lap)
                if e < 2:
                    rolled = pltpu.roll(out, 2 * r, 1)
                    packs[e + 1, hs, :] = jnp.where(
                        (lane_h == 2 * r) | (lane_h == (2 * r + cols - 1) % cols), rolled, packs[e + 1, hs, :])
            return carry

        lax.fori_loop(0, rows, body, 0)

    total_cols = cols * cells_n
    col_f = (lax.broadcasted_iota(jnp.int32, (1, cols), 1) + c * cols)

    def first(r, hs, v, lap):
        flat = (col_f + (w * rows + r) * total_cols).astype(F32)
        cur = (sg[0, hs, :] == flat).astype(F32) - (sg[1, hs, :] == flat).astype(F32)
        out = cur - (LEAK * v + lap)
        f0[r + 1, hs, :] = out
        r0_ref[r, hs, :] = out
        return out

    def second(r, hs, v, lap):
        f1[r + 1, hs, :] = lap
        w1_ref[r, hs, :] = lap
        return lap

    def third(r, hs, v, lap):
        w2_ref[r, hs, :] = lap
        return lap

    def two_rows(ref, i, off):
        return split(jnp.concatenate([ref[2 * i + off], ref[2 * i + 1 + off]], 1))

    nst = len(stages)
    gl = bufs[:nst + 1]
    rb = bufs[nst + 1:]
    offs = [sum(pieces[:k]) for k in range(len(pieces))]

    def reduce_start(s, k):
        g, _ = stages[s]
        n = pieces[k] // g
        for o in range(1, g):
            other, rk = peer(s, o)
            pltpu.make_async_remote_copy(
                src_ref=gl[s].at[pl.ds(pl.multiple_of(offs[k] + other * n, 8), n)],
                dst_ref=rb[s * len(pieces) + k].at[o - 1],
                send_sem=gsend.at[s, k, 0], recv_sem=grecv.at[s, k, 0],
                device_id=dev(rk), device_id_type=MESH).start()

    def wait_all(s, k, phase):
        buf = rb[s * len(pieces) + k]
        pltpu.make_async_copy(buf, buf, gsend.at[s, k, phase]).wait()
        pltpu.make_async_copy(buf, buf, grecv.at[s, k, phase]).wait()

    def reduce_finish(s, k):
        g, stride = stages[s]
        n = pieces[k] // g
        wait_all(s, k, 0)
        me = (rank // stride) % g
        mine = pl.ds(pl.multiple_of(offs[k] + me * n, 8), n)
        total = gl[s][mine, :]
        for o in range(g - 1):
            total = total + rb[s * len(pieces) + k][o]
        gl[s + 1][mine, :] = total
        for o in range(1, g):
            _, rk = peer(s, o)
            pltpu.make_async_remote_copy(
                src_ref=gl[s + 1].at[mine], dst_ref=gl[s + 1].at[mine],
                send_sem=gsend.at[s, k, 1], recv_sem=grecv.at[s, k, 1],
                device_id=dev(rk), device_id_type=MESH).start()

    wait(ex[0])
    stencil(0, first)
    start(ex[1])

    def gram0(i, acc):
        a = two_rows(f0, i, 1)
        return acc + dot3(a, a, NT)

    gl[0][0:pairs, :] = lax.fori_loop(0, rows // 2, gram0, jnp.zeros((pairs, pairs), F32))
    reduce_start(0, 0)
    wait(ex[1])
    stencil(1, second)
    start(ex[2])

    def gram1(i, acc):
        a, b = two_rows(f0, i, 1), two_rows(f1, i, 1)
        both = tuple(jnp.concatenate([p, q], 0) for p, q in zip(a, b))
        return acc + dot3(both, b, NT)

    reduce_finish(0, 0)
    gl[0][pairs:3 * pairs, :] = lax.fori_loop(0, rows // 2, gram1, jnp.zeros((2 * pairs, pairs), F32))
    reduce_start(0, 1)
    wait(ex[2])
    stencil(2, third)

    def gram2(i, acc):
        return acc + dot3(two_rows(f1, i, 1), two_rows(w2_ref, i, 0), NT)

    gl[0][3 * pairs:, :] = lax.fori_loop(0, rows // 2, gram2, jnp.zeros((pairs, pairs), F32))
    reduce_start(0, 2)
    reduce_finish(0, 1)
    reduce_finish(0, 2)
    for k in range(3):
        wait_all(0, k, 1)
    for s in range(1, nst):
        for k in range(3):
            reduce_start(s, k)
        for k in range(3):
            reduce_finish(s, k)
        for k in range(3):
            wait_all(s, k, 1)
    gram_ref[...] = gl[nst][...]


def mm(a, b):
    return lax.dot_general(a, b, NN, precision=lax.Precision.HIGHEST, preferred_element_type=F32)


def eliminate(systems):
    n = systems[0][0].shape[0]
    state = [list(s) for s in systems]
    lane = lax.broadcasted_iota(jnp.int32, (n, n), 1)
    row = lax.broadcasted_iota(jnp.int32, (n, n), 0)
    sub = lax.broadcasted_iota(jnp.int32, (BLOCK, n), 0)
    for k in range(n // BLOCK):
        lo, hi = k * BLOCK, (k + 1) * BLOCK
        inside = (row >= lo) & (row < hi)
        lhs_mask = (lane >= lo) & (lane < hi) & jnp.logical_not(inside)
        panels = []
        for mats in state:
            pan = [m[lo:hi, :] for m in mats]
            panels.append(([jnp.broadcast_to(pan[0][:, lo + j:lo + j + 1], (BLOCK, n)) for j in range(BLOCK)], pan))
        for i in range(BLOCK):
            for cs, pan in panels:
                f = cs[i]
                rinv = 1.0 / f[i:i + 1, :]

                def step(t):
                    top = t[i:i + 1, :] * rinv
                    return jnp.where(sub == i, top, t - f * top)

                for j in range(i + 1, BLOCK):
                    cs[j] = step(cs[j])
                for q in range(len(pan)):
                    pan[q] = step(pan[q])
        for mats, (_, pan) in zip(state, panels):
            lhs = jnp.where(lhs_mask, mats[0], 0.0)
            for q in range(len(mats)):
                parts = []
                if lo:
                    parts.append(jnp.zeros((lo, n), F32))
                parts.append(pan[q])
                if hi < n:
                    parts.append(jnp.zeros((n - hi, n), F32))
                full = jnp.concatenate(parts, 0)
                mats[q] = jnp.where(inside, full, mats[q] - mm(lhs, full))
    return [s[1:] for s in state]


def finish_kernel(gram_ref, r0_ref, w1_ref, w2_ref, x_ref, out_x, out_r, ch, cl):
    rows, n, cols = r0_ref.shape

    def sym(m):
        return 0.5 * (m + m.T)

    g = sym(gram_ref[0:n, :])
    e = sym(gram_ref[n:2 * n, :])
    f = sym(gram_ref[2 * n:3 * n, :])
    h = sym(gram_ref[3 * n:, :])
    eye = (lax.broadcasted_iota(jnp.int32, (n, n), 0) == lax.broadcasted_iota(jnp.int32, (n, n), 1)).astype(F32)
    (a, ap), (ginv,) = eliminate([(LEAK * g + e, g, e), (g, eye)])
    rr = sym(mm(a.T, mm(f, a) - mm(e, ap)))
    p = ap + mm(ginv, rr)
    curv = sym(mm(a.T, mm(LEAK * f + h, a) - mm(LEAK * e + f, p)))
    ((al,),) = eliminate([(curv, rr)])
    q = mm(a, al)
    pq = mm(p, al)
    zero = jnp.zeros((n, n), F32)
    top = jnp.concatenate([(a + pq).T, -q.T, zero], 1)
    bottom = jnp.concatenate([(ap - LEAK * pq).T, (LEAK * q - a - pq).T, q.T], 1)
    hi, lo = split(jnp.concatenate([top, bottom], 0))
    ch[...] = hi
    cl[...] = lo

    def body(i, carry):
        fh, fl = split(jnp.concatenate(
            [jnp.concatenate([ref[2 * i], ref[2 * i + 1]], 1) for ref in (r0_ref, w1_ref, w2_ref)], 0))
        out = dot3((ch[...], cl[...]), (fh, fl), NN)
        for d in range(2):
            at = pl.ds(2 * i + d, n, stride=rows)
            out_x[at, :] = x_ref[at, :] + out[:n, d * cols:(d + 1) * cols]
            out_r[at, :] = out[n:, d * cols:(d + 1) * cols]
        return carry

    lax.fori_loop(0, rows // 2, body, 0)


def per_device(sizes, land_cover, prune_mask, class_resistance, source_cells, ground_cells, warm_start):
    rows, cols = land_cover.shape
    pairs = warm_start.shape[0]
    pieces = (pairs, 2 * pairs, pairs)
    count = sizes[0] * sizes[1] * sizes[2]
    stages = stages_of(count)
    nst = max(1, len(stages))
    x2d = warm_start.reshape(pairs * rows, cols)
    field = jax.ShapeDtypeStruct((rows, pairs, cols), F32)
    vm = pl.BlockSpec(memory_space=pltpu.VMEM)
    sums = [pltpu.VMEM((4 * pairs, pairs), F32) for _ in range(nst + 1)]
    slots = [pltpu.VMEM((g - 1, n // g, pairs), F32) for g, _ in stages for n in pieces]
    r0, w1, w2, gram = pl.pallas_call(
        functools.partial(krylov_kernel, sizes, pieces),
        out_shape=(field, field, field, jax.ShapeDtypeStruct((4 * pairs, pairs), F32)),
        in_specs=[vm, vm, pl.BlockSpec(memory_space=pltpu.SMEM), vm, vm, vm],
        out_specs=(vm, vm, vm, vm),
        scratch_shapes=[
            pltpu.VMEM((rows + 2, pairs, cols), F32),
            pltpu.VMEM((rows + 2, pairs, cols), F32),
            pltpu.VMEM((rows + 2, pairs, cols), F32),
            pltpu.VMEM((3, pairs, cols), F32),
            pltpu.VMEM((3, pairs, cols), F32),
            pltpu.VMEM((3, pairs, cols), F32),
            pltpu.VMEM((8, cols), F32),
            pltpu.VMEM((8, cols), F32),
            pltpu.VMEM((8, cols), F32),
            pltpu.VMEM((2, rows, cols), F32),
            pltpu.VMEM((2, rows, cols), F32),
            pltpu.VMEM((2, rows, cols), F32),
            pltpu.VMEM((4, rows, cols), F32),
            pltpu.VMEM((2, pairs, cols), F32),
            pltpu.SemaphoreType.DMA((3, 4)),
            pltpu.SemaphoreType.DMA((3, 4)),
            pltpu.SemaphoreType.DMA((4,)),
            pltpu.SemaphoreType.DMA((4,)),
            pltpu.SemaphoreType.DMA((nst, 3, 2)),
            pltpu.SemaphoreType.DMA((nst, 3, 2)),
            *sums, *slots,
        ],
        compiler_params=pltpu.CompilerParams(
            collective_id=0, has_side_effects=True, vmem_limit_bytes=40 * 2**20),
        name="krylov",
    )(land_cover, prune_mask, class_resistance, source_cells.reshape(1, pairs), ground_cells.reshape(1, pairs), x2d)
    flat = jax.ShapeDtypeStruct((pairs * rows, cols), F32)
    pot, resid = pl.pallas_call(
        finish_kernel,
        out_shape=(flat, flat),
        in_specs=[vm] * 5,
        out_specs=(vm, vm),
        scratch_shapes=[pltpu.VMEM((2 * pairs, 3 * pairs), jnp.bfloat16)] * 2,
        compiler_params=pltpu.CompilerParams(vmem_limit_bytes=40 * 2**20),
        name="finish",
    )(gram, r0, w1, w2, x2d)
    return pot.reshape(warm_start.shape), resid.reshape(warm_start.shape)


def solution(mesh):
    in_specs = (
        P(("groups", "wide"), ("narrow", "inner")),
        P(None, ("groups", "wide"), ("narrow", "inner")),
        P(),
        P("groups"),
        P("groups"),
        P(None, ("groups", "wide"), ("narrow", "inner")),
    )
    out_specs = (
        P(None, ("groups", "wide"), ("narrow", "inner")),
        P(None, ("groups", "wide"), ("narrow", "inner")),
    )
    sizes = tuple(mesh.shape[a] for a in ("wide", "narrow", "inner"))
    return jax.shard_map(
        functools.partial(per_device, sizes), mesh=mesh, in_specs=in_specs, out_specs=out_specs, check_vma=False
    )
```

```python
import functools
import jax
import jax.numpy as jnp
from jax import lax
from jax.experimental import pallas as pl
from jax.experimental.pallas import tpu as pltpu
from jax.sharding import PartitionSpec as P

LEAK = 0.1
MESH = pl.DeviceIdType.MESH
F32 = jnp.float32
GROUP = 16
BLOCK = 16
STEP = 4
NT = (((1,), (1,)), ((), ()))
NN = (((1,), (0,)), ((), ()))


def split(x):
    hi = x.astype(jnp.bfloat16)
    return hi, (x - hi.astype(F32)).astype(jnp.bfloat16)


def dot3(a, b, dims):
    (ah, al), (bh, bl) = a, b
    mm = functools.partial(lax.dot_general, dimension_numbers=dims, preferred_element_type=F32)
    return mm(ah, bh) + (mm(ah, bl) + mm(al, bh))


def stages_of(count):
    out, stride = [], 1
    while count > 1:
        g = min(GROUP, count)
        assert count % g == 0
        out.append((g, stride))
        stride *= g
        count //= g
    return out


def krylov_kernel(sizes, pieces, cover_hbm, prune_hbm, table_hbm, src_hbm, gnd_hbm, x_hbm,
                  vh, vl, gram_ref,
                  cover_ref, prune_ref, table_ref, src_ref, gnd_ref, x_ref, insem, fx, f0, f1, packs, lefts, rights, edge, edge_up, edge_down, side, side_left, side_right,
                  cond, sg, hsend, hrecv, isend, irecv, gsend, grecv, *bufs):
    wide_n, narrow_n, inner_n = sizes
    pairs = fx.shape[1]
    rows, cols = cover_ref.shape
    cells_n = narrow_n * inner_n
    stages = stages_of(wide_n * cells_n)
    w = lax.axis_index("wide")
    c = lax.axis_index("narrow") * inner_n + lax.axis_index("inner")
    rank = w * cells_n + c

    def dev(rk):
        return {"wide": rk // cells_n, "narrow": (rk % cells_n) // inner_n, "inner": rk % inner_n}

    has_up, has_down = w > 0, w < wide_n - 1
    has_left, has_right = c > 0, c < cells_n - 1
    sides = ((has_up, rank - cells_n), (has_down, rank + cells_n), (has_left, rank - 1), (has_right, rank + 1))

    def peer(stage, o):
        g, stride = stages[stage]
        digit = (rank // stride) % g
        other = (digit + o) % g
        return other, rank + (other - digit) * stride

    loads = [pltpu.make_async_copy(a, b, insem.at[i]) for i, (a, b) in enumerate((
        (x_hbm, x_ref), (cover_hbm, cover_ref), (prune_hbm, prune_ref), (table_hbm, table_ref),
        (src_hbm, src_ref), (gnd_hbm, gnd_ref)))]
    for cp in loads:
        cp.start()
    barrier = pltpu.get_barrier_semaphore()
    expect = 0
    for s, (g, _) in enumerate(stages):
        for o in range(1, g):
            pl.semaphore_signal(barrier, inc=1, device_id=dev(peer(s, o)[1]), device_id_type=MESH)
            expect += 1
    near = 0
    if len(stages) > 1:
        for has, rk in sides:
            near = near + has.astype(jnp.int32)

            @pl.when(has)
            def _(rk=rk):
                pl.semaphore_signal(barrier, inc=1, device_id=dev(rk), device_id_type=MESH)

    lane = lax.broadcasted_iota(jnp.int32, (pairs, cols), 1)
    half = pairs // 2
    lane_h = lax.broadcasted_iota(jnp.int32, (half, cols), 1)

    for cp in loads[1:4]:
        cp.wait()
    cover = cover_ref[...]
    res = jnp.zeros((rows, cols), F32)
    for k in range(table_ref.shape[0]):
        res = jnp.where(cover == k, table_ref[k], res)
    keep_r = (1 - prune_ref[0]).astype(F32)
    keep_d = (1 - prune_ref[1]).astype(F32)
    side[0] = res
    side[1] = keep_r
    edge[...] = jnp.concatenate([res[:1], res[rows - 1:], keep_d[rows - 1:], res[: 5]], 0)

    zero_row = jnp.zeros((pairs, cols), F32)
    for has, bufs0 in ((has_up, tuple(f.at[0] for f in (fx, f0, f1))),
                       (has_down, tuple(f.at[rows + 1] for f in (fx, f0, f1))),
                       (has_left, tuple(lefts.at[e] for e in range(3))),
                       (has_right, tuple(rights.at[e] for e in range(3)))):
        @pl.when(jnp.logical_not(has))
        def _(bufs0=bufs0):
            for b in bufs0:
                b[...] = zero_row

    for has, ref in ((has_up, edge_up), (has_down, edge_down), (has_left, side_left), (has_right, side_right)):
        @pl.when(jnp.logical_not(has))
        def _(ref=ref):
            ref[...] = jnp.ones(ref.shape, F32)

    packs[0] = zero_row
    loads[0].wait()

    def load_rows(i, carry):
        pack = packs[0]
        for d in range(STEP):
            r = i * STEP + d
            v = x_ref[pl.ds(r, pairs, stride=rows), :]
            fx[r + 1] = v
            rolled = pltpu.roll(v, 2 * r, 1)
            pack = jnp.where((lane == 2 * r) | (lane == (2 * r + cols - 1) % cols), rolled, pack)
        packs[0] = pack
        return carry

    lax.fori_loop(0, rows // STEP, load_rows, 0)
    pl.semaphore_wait(barrier, expect + near)

    def halo(e):
        field = (fx, f0, f1)[e]
        return (
            (field.at[1], field.at[rows + 1], 0),
            (field.at[rows], field.at[0], 1),
            (packs.at[e], rights.at[e], 2),
            (packs.at[e], lefts.at[e], 3),
        )

    def copies(items, ssem, rsem):
        out = []
        for (src, dst, k), (has, rk) in zip(items, sides):
            out.append((has, pltpu.make_async_remote_copy(
                src_ref=src, dst_ref=dst, send_sem=ssem.at[k], recv_sem=rsem.at[k],
                device_id=dev(rk), device_id_type=MESH)))
        return out

    def start(cs):
        for has, cp in cs:
            @pl.when(has)
            def _(cp=cp):
                cp.start()

    def wait(cs):
        order = (1, 0, 3, 2)
        for k, (has, cp) in enumerate(cs):
            @pl.when(has)
            def _(cp=cp):
                cp.wait_send()

            @pl.when(cs[order[k]][0])
            def _(cp=cp):
                cp.wait_recv()

    info = copies(((edge, edge_down, 0), (edge, edge_up, 1), (side, side_right, 2), (side, side_left, 3)), isend, irecv)
    start(info)
    ex = [copies(halo(e), hsend.at[e], hrecv.at[e]) for e in range(3)]
    start(ex[0])

    for cp in loads[4:]:
        cp.wait()
    src_t = jnp.broadcast_to(src_ref[...].astype(F32), (cols, pairs)).T
    gnd_t = jnp.broadcast_to(gnd_ref[...].astype(F32), (cols, pairs)).T
    sg[0] = src_t
    sg[1] = gnd_t

    wait(info)
    lane_r = lax.broadcasted_iota(jnp.int32, (rows, cols), 1)
    row_r = lax.broadcasted_iota(jnp.int32, (rows, cols), 0)
    right_res = jnp.where(lane_r == cols - 1, pltpu.roll(side_right[0], cols - 1, 1), pltpu.roll(res, cols - 1, 1))
    left_res = jnp.where(lane_r == 0, pltpu.roll(side_left[0], 1, 1), pltpu.roll(res, 1, 1))
    left_keep = jnp.where(lane_r == 0, pltpu.roll(side_left[1], 1, 1), pltpu.roll(keep_r, 1, 1))
    down_res = jnp.where(row_r == rows - 1, edge_down[0:1, :], pltpu.roll(res, rows - 1, 0))
    up_res = jnp.where(row_r == 0, edge_up[1:2, :], pltpu.roll(res, 1, 0))
    up_keep = jnp.where(row_r == 0, edge_up[2:3, :], pltpu.roll(keep_d, 1, 0))
    at_right = (lane_r == cols - 1) & jnp.logical_not(has_right)
    at_left = (lane_r == 0) & jnp.logical_not(has_left)
    at_down = (row_r == rows - 1) & jnp.logical_not(has_down)
    at_up = (row_r == 0) & jnp.logical_not(has_up)
    cond[0] = jnp.where(at_right, 0.0, keep_r * 2.0 / (res + right_res))
    cond[1] = jnp.where(at_left, 0.0, left_keep * 2.0 / (res + left_res))
    cond[2] = jnp.where(at_down, 0.0, keep_d * 2.0 / (res + down_res))
    cond[3] = jnp.where(at_up, 0.0, up_keep * 2.0 / (res + up_res))

    def stencil(e, finish):
        field = (fx, f0, f1)[e]
        even = (lane % 2) == 0
        lefts[e] = jnp.where(even, rights[e], pltpu.roll(lefts[e], 2, 1))
        if e < 2:
            packs[e + 1] = zero_row

        def body(i, carry):
            for h in range(2):
                hs = pl.ds(h * half, half)
                halos = lefts[e, hs, :]
                pack = packs[e + 1, hs, :] if e < 2 else None
                for d in range(STEP):
                    r = i * STEP + d
                    cr, cl, cd, cu = (cond[k, pl.ds(r, 1), :] for k in range(4))
                    v = field[r + 1, hs, :]
                    edges = pltpu.roll(halos, (2 * cols - 2 * r - 1) % cols, 1)
                    xr = jnp.where(lane_h == cols - 1, edges, pltpu.roll(v, cols - 1, 1))
                    xl = jnp.where(lane_h == 0, edges, pltpu.roll(v, 1, 1))
                    lap = cr * (v - xr) + cl * (v - xl) + cd * (v - field[r + 2, hs, :]) + cu * (v - field[r, hs, :])
                    out = finish(r, hs, v, lap)
                    if e < 2:
                        (f0, f1)[e][r + 1, hs, :] = out
                        rolled = pltpu.roll(out, 2 * r, 1)
                        pack = jnp.where(
                            (lane_h == 2 * r) | (lane_h == (2 * r + cols - 1) % cols), rolled, pack)
                    at = (pl.ds(e * pairs + h * half, half), pl.ds(pl.multiple_of(r * cols, cols), cols))
                    hi, lo = split(out)
                    vh[at] = hi
                    vl[at] = lo
                if e < 2:
                    packs[e + 1, hs, :] = pack
            return carry

        lax.fori_loop(0, rows // STEP, body, 0)

    total_cols = cols * cells_n
    col_f = (lax.broadcasted_iota(jnp.int32, (1, cols), 1) + c * cols)

    def first(r, hs, v, lap):
        flat = (col_f + (w * rows + r) * total_cols).astype(F32)
        cur = (sg[0, hs, :] == flat).astype(F32) - (sg[1, hs, :] == flat).astype(F32)
        out = cur - (LEAK * v + lap)
        return out

    def second(r, hs, v, lap):
        return lap

    def part(lo, hi):
        return vh[lo * pairs:hi * pairs, :], vl[lo * pairs:hi * pairs, :]

    nst = len(stages)
    gl = bufs[:nst + 1]
    rb = bufs[nst + 1:]
    offs = [sum(pieces[:k]) for k in range(len(pieces))]

    def reduce_start(s, k):
        g, _ = stages[s]
        n = pieces[k] // g
        for o in range(1, g):
            other, rk = peer(s, o)
            pltpu.make_async_remote_copy(
                src_ref=gl[s].at[pl.ds(pl.multiple_of(offs[k] + other * n, 8), n)],
                dst_ref=rb[s * len(pieces) + k].at[o - 1],
                send_sem=gsend.at[s, k, 0], recv_sem=grecv.at[s, k, 0],
                device_id=dev(rk), device_id_type=MESH).start()

    def wait_all(s, k, phase):
        buf = rb[s * len(pieces) + k]
        pltpu.make_async_copy(buf, buf, gsend.at[s, k, phase]).wait()
        pltpu.make_async_copy(buf, buf, grecv.at[s, k, phase]).wait()

    def reduce_finish(s, k):
        g, stride = stages[s]
        n = pieces[k] // g
        wait_all(s, k, 0)
        me = (rank // stride) % g
        mine = pl.ds(pl.multiple_of(offs[k] + me * n, 8), n)
        total = gl[s][mine, :]
        for o in range(g - 1):
            total = total + rb[s * len(pieces) + k][o]
        gl[s + 1][mine, :] = total
        for o in range(1, g):
            _, rk = peer(s, o)
            pltpu.make_async_remote_copy(
                src_ref=gl[s + 1].at[mine], dst_ref=gl[s + 1].at[mine],
                send_sem=gsend.at[s, k, 1], recv_sem=grecv.at[s, k, 1],
                device_id=dev(rk), device_id_type=MESH).start()

    wait(ex[0])
    stencil(0, first)
    start(ex[1])

    gl[0][0:pairs, :] = dot3(part(0, 1), part(0, 1), NT)
    reduce_start(0, 0)
    wait(ex[1])
    stencil(1, second)
    start(ex[2])

    reduce_finish(0, 0)
    gl[0][pairs:3 * pairs, :] = dot3(part(0, 2), part(1, 2), NT)
    reduce_start(0, 1)
    wait(ex[2])
    stencil(2, second)

    gl[0][3 * pairs:, :] = dot3(part(1, 2), part(2, 3), NT)
    reduce_start(0, 2)
    reduce_finish(0, 1)
    reduce_finish(0, 2)
    for k in range(3):
        wait_all(0, k, 1)
    for s in range(1, nst):
        for k in range(3):
            reduce_start(s, k)
        for k in range(3):
            reduce_finish(s, k)
        for k in range(3):
            wait_all(s, k, 1)
    gram_ref[...] = gl[nst][...]


def mm(a, b):
    return lax.dot_general(a, b, NN, precision=lax.Precision.HIGHEST, preferred_element_type=F32)


def eliminate(systems):
    n = systems[0][0].shape[0]
    state = [list(s) for s in systems]
    lane = lax.broadcasted_iota(jnp.int32, (n, n), 1)
    row = lax.broadcasted_iota(jnp.int32, (n, n), 0)
    sub = lax.broadcasted_iota(jnp.int32, (BLOCK, n), 0)
    for k in range(n // BLOCK):
        lo, hi = k * BLOCK, (k + 1) * BLOCK
        inside = (row >= lo) & (row < hi)
        lhs_mask = (lane >= lo) & (lane < hi) & jnp.logical_not(inside)
        panels = []
        for mats in state:
            pan = [m[lo:hi, :] for m in mats]
            panels.append(([jnp.broadcast_to(pan[0][:, lo + j:lo + j + 1], (BLOCK, n)) for j in range(BLOCK)], pan))
        for i in range(BLOCK):
            for cs, pan in panels:
                f = cs[i]
                rinv = 1.0 / f[i:i + 1, :]

                def step(t):
                    top = t[i:i + 1, :] * rinv
                    return jnp.where(sub == i, top, t - f * top)

                for j in range(i + 1, BLOCK):
                    cs[j] = step(cs[j])
                for q in range(len(pan)):
                    pan[q] = step(pan[q])
        for mats, (_, pan) in zip(state, panels):
            lhs = jnp.where(lhs_mask, mats[0], 0.0)
            for q in range(len(mats)):
                parts = []
                if lo:
                    parts.append(jnp.zeros((lo, n), F32))
                parts.append(pan[q])
                if hi < n:
                    parts.append(jnp.zeros((n - hi, n), F32))
                full = jnp.concatenate(parts, 0)
                mats[q] = jnp.where(inside, full, mats[q] - mm(lhs, full))
    return [s[1:] for s in state]


def finish_kernel(gram_ref, vh, vl, x_hbm, out_x, out_r, x_ref, bx, br, ch, cl, insem, outsem):
    groups, n, tile, cols = bx.shape
    rows = groups * tile
    load = pltpu.make_async_copy(x_hbm, x_ref, insem)
    load.start()

    def sym(m):
        return 0.5 * (m + m.T)

    g = sym(gram_ref[0:n, :])
    e = sym(gram_ref[n:2 * n, :])
    f = sym(gram_ref[2 * n:3 * n, :])
    h = sym(gram_ref[3 * n:, :])
    eye = (lax.broadcasted_iota(jnp.int32, (n, n), 0) == lax.broadcasted_iota(jnp.int32, (n, n), 1)).astype(F32)
    (a, ap), (ginv,) = eliminate([(LEAK * g + e, g, e), (g, eye)])
    rr = sym(mm(a.T, mm(f, a) - mm(e, ap)))
    p = ap + mm(ginv, rr)
    curv = sym(mm(a.T, mm(LEAK * f + h, a) - mm(LEAK * e + f, p)))
    ((al,),) = eliminate([(curv, rr)])
    q = mm(a, al)
    pq = mm(p, al)
    zero = jnp.zeros((n, n), F32)
    top = jnp.concatenate([(a + pq).T, -q.T, zero], 1)
    bottom = jnp.concatenate([(ap - LEAK * pq).T, (LEAK * q - a - pq).T, q.T], 1)
    hi, lo = split(jnp.concatenate([top, bottom], 0))
    ch[...] = hi
    cl[...] = lo

    load.wait()
    stores = []
    for g in range(groups):
        for i in range(tile // 2):
            at = pl.ds((g * tile + 2 * i) * cols, 2 * cols)
            out = dot3((ch[...], cl[...]), (vh[:, at], vl[:, at]), NN)
            for d in range(2):
                r = 2 * i + d
                here = pl.ds(r, n, stride=tile)
                bx.at[g].reshape(n * tile, cols)[here, :] = (
                    x_ref[pl.ds(g * tile + r, n, stride=rows), :] + out[:n, d * cols:(d + 1) * cols])
                br.at[g].reshape(n * tile, cols)[here, :] = out[n:, d * cols:(d + 1) * cols]
        for j, (buf, dst) in enumerate(((bx, out_x), (br, out_r))):
            cp = pltpu.make_async_copy(buf.at[g], dst.at[:, pl.ds(g * tile, tile), :], outsem.at[j, g])
            cp.start()
            stores.append(cp)
    for cp in stores:
        cp.wait()


def per_device(sizes, land_cover, prune_mask, class_resistance, source_cells, ground_cells, warm_start):
    rows, cols = land_cover.shape
    pairs = warm_start.shape[0]
    pieces = (pairs, 2 * pairs, pairs)
    count = sizes[0] * sizes[1] * sizes[2]
    stages = stages_of(count)
    nst = max(1, len(stages))
    x2d = warm_start.reshape(pairs * rows, cols)
    basis = jax.ShapeDtypeStruct((3 * pairs, rows * cols), jnp.bfloat16)
    hbm = pl.BlockSpec(memory_space=pltpu.HBM)
    vm = pl.BlockSpec(memory_space=pltpu.VMEM)
    sums = [pltpu.VMEM((4 * pairs, pairs), F32) for _ in range(nst + 1)]
    slots = [pltpu.VMEM((g - 1, n // g, pairs), F32) for g, _ in stages for n in pieces]
    vh, vl, gram = pl.pallas_call(
        functools.partial(krylov_kernel, sizes, pieces),
        out_shape=(basis, basis, jax.ShapeDtypeStruct((4 * pairs, pairs), F32)),
        in_specs=[hbm] * 6,
        out_specs=(vm, vm, vm),
        scratch_shapes=[
            pltpu.VMEM((rows, cols), jnp.int32),
            pltpu.VMEM((2, rows, cols), jnp.int32),
            pltpu.SMEM(class_resistance.shape, F32),
            pltpu.VMEM((1, pairs), jnp.int32),
            pltpu.VMEM((1, pairs), jnp.int32),
            pltpu.VMEM((pairs * rows, cols), F32),
            pltpu.SemaphoreType.DMA((6,)),
            pltpu.VMEM((rows + 2, pairs, cols), F32),
            pltpu.VMEM((rows + 2, pairs, cols), F32),
            pltpu.VMEM((rows + 2, pairs, cols), F32),
            pltpu.VMEM((3, pairs, cols), F32),
            pltpu.VMEM((3, pairs, cols), F32),
            pltpu.VMEM((3, pairs, cols), F32),
            pltpu.VMEM((8, cols), F32),
            pltpu.VMEM((8, cols), F32),
            pltpu.VMEM((8, cols), F32),
            pltpu.VMEM((2, rows, cols), F32),
            pltpu.VMEM((2, rows, cols), F32),
            pltpu.VMEM((2, rows, cols), F32),
            pltpu.VMEM((4, rows, cols), F32),
            pltpu.VMEM((2, pairs, cols), F32),
            pltpu.SemaphoreType.DMA((3, 4)),
            pltpu.SemaphoreType.DMA((3, 4)),
            pltpu.SemaphoreType.DMA((4,)),
            pltpu.SemaphoreType.DMA((4,)),
            pltpu.SemaphoreType.DMA((nst, 3, 2)),
            pltpu.SemaphoreType.DMA((nst, 3, 2)),
            *sums, *slots,
        ],
        compiler_params=pltpu.CompilerParams(
            collective_id=0, has_side_effects=True, vmem_limit_bytes=40 * 2**20),
        name="krylov",
    )(land_cover, prune_mask, class_resistance, source_cells.reshape(1, pairs), ground_cells.reshape(1, pairs), x2d)
    full = jax.ShapeDtypeStruct(warm_start.shape, F32)
    tile = 8
    return pl.pallas_call(
        finish_kernel,
        out_shape=(full, full),
        in_specs=[vm, vm, vm, hbm],
        out_specs=(hbm, hbm),
        scratch_shapes=[
            pltpu.VMEM((pairs * rows, cols), F32),
            pltpu.VMEM((rows // tile, pairs, tile, cols), F32),
            pltpu.VMEM((rows // tile, pairs, tile, cols), F32),
            pltpu.VMEM((2 * pairs, 3 * pairs), jnp.bfloat16),
            pltpu.VMEM((2 * pairs, 3 * pairs), jnp.bfloat16),
            pltpu.SemaphoreType.DMA,
            pltpu.SemaphoreType.DMA((2, rows // tile)),
        ],
        compiler_params=pltpu.CompilerParams(vmem_limit_bytes=40 * 2**20),
        name="finish",
    )(gram, vh, vl, x2d)


def solution(mesh):
    in_specs = (
        P(("groups", "wide"), ("narrow", "inner")),
        P(None, ("groups", "wide"), ("narrow", "inner")),
        P(),
        P("groups"),
        P("groups"),
        P(None, ("groups", "wide"), ("narrow", "inner")),
    )
    out_specs = (
        P(None, ("groups", "wide"), ("narrow", "inner")),
        P(None, ("groups", "wide"), ("narrow", "inner")),
    )
    sizes = tuple(mesh.shape[a] for a in ("wide", "narrow", "inner"))
    return jax.shard_map(
        functools.partial(per_device, sizes), mesh=mesh, in_specs=in_specs, out_specs=out_specs, check_vma=False
    )
```

```python
import functools
import jax
import jax.numpy as jnp
from jax import lax
from jax.experimental import pallas as pl
from jax.experimental.pallas import tpu as pltpu
from jax.sharding import PartitionSpec as P

LEAK = 0.1
MESH = pl.DeviceIdType.MESH
F32 = jnp.float32
GROUP = 16
BLOCK = 16
STEP = 4
NT = (((1,), (1,)), ((), ()))
NN = (((1,), (0,)), ((), ()))


def split(x):
    hi = x.astype(jnp.bfloat16)
    return hi, (x - hi.astype(F32)).astype(jnp.bfloat16)


def dot3(a, b, dims):
    (ah, al), (bh, bl) = a, b
    mm = functools.partial(lax.dot_general, dimension_numbers=dims, preferred_element_type=F32)
    return mm(ah, bh) + (mm(ah, bl) + mm(al, bh))


def stages_of(count):
    out, stride = [], 1
    while count > 1:
        g = min(GROUP, count)
        assert count % g == 0
        out.append((g, stride))
        stride *= g
        count //= g
    return out


def krylov_kernel(sizes, pieces, cover_hbm, prune_hbm, table_hbm, src_hbm, gnd_hbm, x_hbm,
                  vh, vl, gram_ref,
                  cover_ref, prune_ref, table_ref, src_ref, gnd_ref, x_ref, insem, fx, f0, f1, packs, lefts, rights, edge, edge_up, edge_down, side, side_left, side_right,
                  cond, sg, hsend, hrecv, isend, irecv, gsend, grecv, *bufs):
    wide_n, narrow_n, inner_n = sizes
    pairs = fx.shape[1]
    rows, cols = cover_ref.shape
    cells_n = narrow_n * inner_n
    stages = stages_of(wide_n * cells_n)
    w = lax.axis_index("wide")
    c = lax.axis_index("narrow") * inner_n + lax.axis_index("inner")
    rank = w * cells_n + c

    def dev(rk):
        return {"wide": rk // cells_n, "narrow": (rk % cells_n) // inner_n, "inner": rk % inner_n}

    has_up, has_down = w > 0, w < wide_n - 1
    has_left, has_right = c > 0, c < cells_n - 1
    sides = ((has_up, rank - cells_n), (has_down, rank + cells_n), (has_left, rank - 1), (has_right, rank + 1))

    def peer(stage, o):
        g, stride = stages[stage]
        digit = (rank // stride) % g
        other = (digit + o) % g
        return other, rank + (other - digit) * stride

    loads = [pltpu.make_async_copy(a, b, insem.at[i]) for i, (a, b) in enumerate((
        (x_hbm, x_ref), (cover_hbm, cover_ref), (prune_hbm, prune_ref), (table_hbm, table_ref),
        (src_hbm, src_ref), (gnd_hbm, gnd_ref)))]
    for cp in loads:
        cp.start()
    barrier = pltpu.get_barrier_semaphore()
    expect = 0
    for s, (g, _) in enumerate(stages):
        for o in range(1, g):
            pl.semaphore_signal(barrier, inc=1, device_id=dev(peer(s, o)[1]), device_id_type=MESH)
            expect += 1
    near = 0
    if len(stages) > 1:
        for has, rk in sides:
            near = near + has.astype(jnp.int32)

            @pl.when(has)
            def _(rk=rk):
                pl.semaphore_signal(barrier, inc=1, device_id=dev(rk), device_id_type=MESH)

    lane = lax.broadcasted_iota(jnp.int32, (pairs, cols), 1)
    half = pairs // 2

    for cp in loads[1:4]:
        cp.wait()
    cover = cover_ref[...]
    res = jnp.zeros((rows, cols), F32)
    for k in range(table_ref.shape[0]):
        res = jnp.where(cover == k, table_ref[k], res)
    keep_r = (1 - prune_ref[0]).astype(F32)
    keep_d = (1 - prune_ref[1]).astype(F32)
    side[0] = res
    side[1] = keep_r
    edge[...] = jnp.concatenate([res[:1], res[rows - 1:], keep_d[rows - 1:], res[: 5]], 0)

    zero_row = jnp.zeros((pairs, cols), F32)
    for has, bufs0 in ((has_up, tuple(f.at[0] for f in (fx, f0, f1))),
                       (has_down, tuple(f.at[rows + 1] for f in (fx, f0, f1))),
                       (has_left, tuple(lefts.at[e] for e in range(3))),
                       (has_right, tuple(rights.at[e] for e in range(3)))):
        @pl.when(jnp.logical_not(has))
        def _(bufs0=bufs0):
            for b in bufs0:
                b[...] = zero_row

    for has, ref in ((has_up, edge_up), (has_down, edge_down), (has_left, side_left), (has_right, side_right)):
        @pl.when(jnp.logical_not(has))
        def _(ref=ref):
            ref[...] = jnp.ones(ref.shape, F32)

    packs[0] = zero_row
    lane_r = lax.broadcasted_iota(jnp.int32, (rows, cols), 1)
    row_r = lax.broadcasted_iota(jnp.int32, (rows, cols), 0)
    cond[5] = ((lane_r == 2 * row_r) | (lane_r == (2 * row_r + cols - 1) % cols)).astype(F32)
    loads[0].wait()

    def load_rows(i, carry):
        pack = packs[0]
        for d in range(STEP):
            r = i * STEP + d
            v = x_ref[pl.ds(r, pairs, stride=rows), :]
            fx[r + 1] = v
            pack = pack + pltpu.roll(v, 2 * r, 1) * cond[5, pl.ds(r, 1), :]
        packs[0] = pack
        return carry

    lax.fori_loop(0, rows // STEP, load_rows, 0)
    pl.semaphore_wait(barrier, expect + near)

    def halo(e):
        field = (fx, f0, f1)[e]
        return (
            (field.at[1], field.at[rows + 1], 0),
            (field.at[rows], field.at[0], 1),
            (packs.at[e], rights.at[e], 2),
            (packs.at[e], lefts.at[e], 3),
        )

    def copies(items, ssem, rsem):
        out = []
        for (src, dst, k), (has, rk) in zip(items, sides):
            out.append((has, pltpu.make_async_remote_copy(
                src_ref=src, dst_ref=dst, send_sem=ssem.at[k], recv_sem=rsem.at[k],
                device_id=dev(rk), device_id_type=MESH)))
        return out

    def start(cs):
        for has, cp in cs:
            @pl.when(has)
            def _(cp=cp):
                cp.start()

    def wait(cs):
        order = (1, 0, 3, 2)
        for k, (has, cp) in enumerate(cs):
            @pl.when(has)
            def _(cp=cp):
                cp.wait_send()

            @pl.when(cs[order[k]][0])
            def _(cp=cp):
                cp.wait_recv()

    info = copies(((edge, edge_down, 0), (edge, edge_up, 1), (side, side_right, 2), (side, side_left, 3)), isend, irecv)
    start(info)
    ex = [copies(halo(e), hsend.at[e], hrecv.at[e]) for e in range(3)]
    start(ex[0])

    for cp in loads[4:]:
        cp.wait()
    src_t = jnp.broadcast_to(src_ref[...].astype(F32), (cols, pairs)).T
    gnd_t = jnp.broadcast_to(gnd_ref[...].astype(F32), (cols, pairs)).T
    sg[0] = src_t
    sg[1] = gnd_t

    wait(info)
    right_res = jnp.where(lane_r == cols - 1, pltpu.roll(side_right[0], cols - 1, 1), pltpu.roll(res, cols - 1, 1))
    left_res = jnp.where(lane_r == 0, pltpu.roll(side_left[0], 1, 1), pltpu.roll(res, 1, 1))
    left_keep = jnp.where(lane_r == 0, pltpu.roll(side_left[1], 1, 1), pltpu.roll(keep_r, 1, 1))
    down_res = jnp.where(row_r == rows - 1, edge_down[0:1, :], pltpu.roll(res, rows - 1, 0))
    up_res = jnp.where(row_r == 0, edge_up[1:2, :], pltpu.roll(res, 1, 0))
    up_keep = jnp.where(row_r == 0, edge_up[2:3, :], pltpu.roll(keep_d, 1, 0))
    at_right = (lane_r == cols - 1) & jnp.logical_not(has_right)
    at_left = (lane_r == 0) & jnp.logical_not(has_left)
    at_down = (row_r == rows - 1) & jnp.logical_not(has_down)
    at_up = (row_r == 0) & jnp.logical_not(has_up)
    to_right = jnp.where(at_right, 0.0, keep_r * 2.0 / (res + right_res))
    to_left = jnp.where(at_left, 0.0, left_keep * 2.0 / (res + left_res))
    cond[0] = jnp.where(lane_r == cols - 1, 0.0, to_right)
    cond[1] = jnp.where(lane_r == 0, 0.0, to_left)
    cond[4] = jnp.where(lane_r == cols - 1, to_right, jnp.where(lane_r == 0, to_left, 0.0))
    cond[2] = jnp.where(at_down, 0.0, keep_d * 2.0 / (res + down_res))
    cond[3] = jnp.where(at_up, 0.0, up_keep * 2.0 / (res + up_res))

    def stencil(e, finish):
        field = (fx, f0, f1)[e]
        even = (lane % 2) == 0
        lefts[e] = jnp.where(even, rights[e], pltpu.roll(lefts[e], 2, 1))
        if e < 2:
            packs[e + 1] = zero_row

        def body(i, carry):
            for h in range(2):
                hs = pl.ds(h * half, half)
                halos = lefts[e, hs, :]
                pack = packs[e + 1, hs, :] if e < 2 else None
                for d in range(STEP):
                    r = i * STEP + d
                    cr, cl, cd, cu, ce, pm = (cond[k, pl.ds(r, 1), :] for k in range(6))
                    v = field[r + 1, hs, :]
                    edges = pltpu.roll(halos, (2 * cols - 2 * r - 1) % cols, 1)
                    xr = pltpu.roll(v, cols - 1, 1)
                    xl = pltpu.roll(v, 1, 1)
                    lap = cr * (v - xr) + cl * (v - xl) + ce * (v - edges) + cd * (v - field[r + 2, hs, :]) + cu * (v - field[r, hs, :])
                    out = finish(r, hs, v, lap)
                    if e < 2:
                        (f0, f1)[e][r + 1, hs, :] = out
                        pack = pack + pltpu.roll(out, 2 * r, 1) * pm
                    at = (pl.ds(e * pairs + h * half, half), pl.ds(pl.multiple_of(r * cols, cols), cols))
                    hi, lo = split(out)
                    vh[at] = hi
                    vl[at] = lo
                if e < 2:
                    packs[e + 1, hs, :] = pack
            return carry

        lax.fori_loop(0, rows // STEP, body, 0)

    total_cols = cols * cells_n
    col_f = (lax.broadcasted_iota(jnp.int32, (1, cols), 1) + c * cols)

    def first(r, hs, v, lap):
        flat = (col_f + (w * rows + r) * total_cols).astype(F32)
        cur = (sg[0, hs, :] == flat).astype(F32) - (sg[1, hs, :] == flat).astype(F32)
        out = cur - (LEAK * v + lap)
        return out

    def second(r, hs, v, lap):
        return lap

    def part(lo, hi):
        return vh[lo * pairs:hi * pairs, :], vl[lo * pairs:hi * pairs, :]

    nst = len(stages)
    gl = bufs[:nst + 1]
    rb = bufs[nst + 1:]
    offs = [sum(pieces[:k]) for k in range(len(pieces))]

    def reduce_start(s, k):
        g, _ = stages[s]
        n = pieces[k] // g
        for o in range(1, g):
            other, rk = peer(s, o)
            pltpu.make_async_remote_copy(
                src_ref=gl[s].at[pl.ds(pl.multiple_of(offs[k] + other * n, 8), n)],
                dst_ref=rb[s * len(pieces) + k].at[o - 1],
                send_sem=gsend.at[s, k, 0], recv_sem=grecv.at[s, k, 0],
                device_id=dev(rk), device_id_type=MESH).start()

    def wait_all(s, k, phase):
        buf = rb[s * len(pieces) + k]
        pltpu.make_async_copy(buf, buf, gsend.at[s, k, phase]).wait()
        pltpu.make_async_copy(buf, buf, grecv.at[s, k, phase]).wait()

    def reduce_finish(s, k):
        g, stride = stages[s]
        n = pieces[k] // g
        wait_all(s, k, 0)
        me = (rank // stride) % g
        mine = pl.ds(pl.multiple_of(offs[k] + me * n, 8), n)
        total = gl[s][mine, :]
        for o in range(g - 1):
            total = total + rb[s * len(pieces) + k][o]
        gl[s + 1][mine, :] = total
        for o in range(1, g):
            _, rk = peer(s, o)
            pltpu.make_async_remote_copy(
                src_ref=gl[s + 1].at[mine], dst_ref=gl[s + 1].at[mine],
                send_sem=gsend.at[s, k, 1], recv_sem=grecv.at[s, k, 1],
                device_id=dev(rk), device_id_type=MESH).start()

    wait(ex[0])
    stencil(0, first)
    start(ex[1])

    gl[0][0:pairs, :] = dot3(part(0, 1), part(0, 1), NT)
    reduce_start(0, 0)
    wait(ex[1])
    stencil(1, second)
    start(ex[2])

    reduce_finish(0, 0)
    gl[0][pairs:3 * pairs, :] = dot3(part(0, 2), part(1, 2), NT)
    reduce_start(0, 1)
    wait(ex[2])
    stencil(2, second)

    reduce_finish(0, 1)
    gl[0][3 * pairs:, :] = dot3(part(1, 2), part(2, 3), NT)
    reduce_start(0, 2)
    reduce_finish(0, 2)
    for k in range(3):
        wait_all(0, k, 1)
    for s in range(1, nst):
        for k in range(3):
            reduce_start(s, k)
        for k in range(3):
            reduce_finish(s, k)
        for k in range(3):
            wait_all(s, k, 1)
    gram_ref[...] = gl[nst][...]


def mm(a, b):
    return lax.dot_general(a, b, NN, precision=lax.Precision.HIGHEST, preferred_element_type=F32)


def split3(x):
    h1 = x.astype(jnp.bfloat16)
    rest = x - h1.astype(F32)
    h2 = rest.astype(jnp.bfloat16)
    return h1, h2, (rest - h2.astype(F32)).astype(jnp.bfloat16)


def eliminate(systems):
    n = systems[0][0].shape[0]
    state = [list(s) for s in systems]
    lane = lax.broadcasted_iota(jnp.int32, (n, n), 1)
    row = lax.broadcasted_iota(jnp.int32, (n, n), 0)
    sub = lax.broadcasted_iota(jnp.int32, (BLOCK, n), 0)
    slot = lane // BLOCK
    second, third = (slot == 2) | (slot == 5), slot == 4
    assert n == 8 * BLOCK
    for k in range(n // BLOCK):
        lo, hi = k * BLOCK, (k + 1) * BLOCK
        inside = (row >= lo) & (row < hi)
        lhs_mask = (lane >= lo) & (lane < hi) & jnp.logical_not(inside)
        panels, lefts = [], []
        for mats in state:
            t = jnp.where(lhs_mask, mats[0], 0.0)
            for shift in (BLOCK, 2 * BLOCK, 4 * BLOCK):
                t = t + pltpu.roll(t, shift, 1)
            h1 = t.astype(jnp.bfloat16).astype(F32)
            h2 = (t - h1).astype(jnp.bfloat16).astype(F32)
            h3 = t - h1 - h2
            lefts.append(jnp.where(third, h3, jnp.where(second, h2, h1)).astype(jnp.bfloat16))
            pan = [m[lo:hi, :] for m in mats]
            panels.append(([jnp.broadcast_to(pan[0][:, lo + j:lo + j + 1], (BLOCK, n)) for j in range(BLOCK)], pan))
        for i in range(BLOCK):
            for cs, pan in panels:
                f = cs[i]
                rinv = 1.0 / f[i:i + 1, :]

                def step(t):
                    top = t[i:i + 1, :] * rinv
                    return jnp.where(sub == i, top, t - f * top)

                for j in range(i + 1, BLOCK):
                    cs[j] = step(cs[j])
                for q in range(len(pan)):
                    pan[q] = step(pan[q])
        for mats, lhs, (_, pan) in zip(state, lefts, panels):
            q1, q2, q3 = split3(jnp.concatenate(pan, 1))
            none = jnp.zeros((n - 6 * BLOCK, q1.shape[1]), jnp.bfloat16)
            rhs = jnp.concatenate([q1, q2, q1, q3, q1, q2, none], 0)
            change = lax.dot_general(lhs, rhs, NN, preferred_element_type=F32)
            for q in range(len(mats)):
                parts = [pan[q]]
                if lo:
                    parts.insert(0, mats[q][:lo] - change[:lo, q * n:(q + 1) * n])
                if hi < n:
                    parts.append(mats[q][hi:] - change[hi:, q * n:(q + 1) * n])
                mats[q] = jnp.concatenate(parts, 0)
    return [s[1:] for s in state]


def finish_kernel(gram_ref, vh, vl, x_hbm, out_x, out_r, x_ref, bx, br, ch, cl, insem, outsem):
    groups, n, tile, cols = bx.shape
    rows = groups * tile
    load = pltpu.make_async_copy(x_hbm, x_ref, insem)
    load.start()

    def sym(m):
        return 0.5 * (m + m.T)

    g = sym(gram_ref[0:n, :])
    e = sym(gram_ref[n:2 * n, :])
    f = sym(gram_ref[2 * n:3 * n, :])
    h = sym(gram_ref[3 * n:, :])
    eye = (lax.broadcasted_iota(jnp.int32, (n, n), 0) == lax.broadcasted_iota(jnp.int32, (n, n), 1)).astype(F32)
    (a, ap), (ginv,) = eliminate([(LEAK * g + e, g, e), (g, eye)])
    rr = sym(mm(a.T, mm(f, a) - mm(e, ap)))
    p = ap + mm(ginv, rr)
    curv = sym(mm(a.T, mm(LEAK * f + h, a) - mm(LEAK * e + f, p)))
    ((al,),) = eliminate([(curv, rr)])
    q = mm(a, al)
    pq = mm(p, al)
    zero = jnp.zeros((n, n), F32)
    top = jnp.concatenate([(a + pq).T, -q.T, zero], 1)
    bottom = jnp.concatenate([(ap - LEAK * pq).T, (LEAK * q - a - pq).T, q.T], 1)
    hi, lo = split(jnp.concatenate([top, bottom], 0))
    ch[...] = hi
    cl[...] = lo

    load.wait()
    stores = []
    for g in range(groups):
        for i in range(tile // 2):
            at = pl.ds((g * tile + 2 * i) * cols, 2 * cols)
            out = dot3((ch[...], cl[...]), (vh[:, at], vl[:, at]), NN)
            for d in range(2):
                r = 2 * i + d
                here = pl.ds(r, n, stride=tile)
                bx.at[g].reshape(n * tile, cols)[here, :] = (
                    x_ref[pl.ds(g * tile + r, n, stride=rows), :] + out[:n, d * cols:(d + 1) * cols])
                br.at[g].reshape(n * tile, cols)[here, :] = out[n:, d * cols:(d + 1) * cols]
        for j, (buf, dst) in enumerate(((bx, out_x), (br, out_r))):
            cp = pltpu.make_async_copy(buf.at[g], dst.at[:, pl.ds(g * tile, tile), :], outsem.at[j, g])
            cp.start()
            stores.append(cp)
    for cp in stores:
        cp.wait()


def per_device(sizes, land_cover, prune_mask, class_resistance, source_cells, ground_cells, warm_start):
    rows, cols = land_cover.shape
    pairs = warm_start.shape[0]
    pieces = (pairs, 2 * pairs, pairs)
    count = sizes[0] * sizes[1] * sizes[2]
    stages = stages_of(count)
    nst = max(1, len(stages))
    x2d, land_cover, prune_mask, class_resistance, source_cells, ground_cells = (
        pltpu.with_memory_space_constraint(v, pltpu.HBM) for v in (
            warm_start.reshape(pairs * rows, cols), land_cover, prune_mask, class_resistance,
            source_cells.reshape(1, pairs), ground_cells.reshape(1, pairs)))
    basis = jax.ShapeDtypeStruct((3 * pairs, rows * cols), jnp.bfloat16)
    hbm = pl.BlockSpec(memory_space=pltpu.HBM)
    vm = pl.BlockSpec(memory_space=pltpu.VMEM)
    sums = [pltpu.VMEM((4 * pairs, pairs), F32) for _ in range(nst + 1)]
    slots = [pltpu.VMEM((g - 1, n // g, pairs), F32) for g, _ in stages for n in pieces]
    vh, vl, gram = pl.pallas_call(
        functools.partial(krylov_kernel, sizes, pieces),
        out_shape=(basis, basis, jax.ShapeDtypeStruct((4 * pairs, pairs), F32)),
        in_specs=[hbm] * 6,
        out_specs=(vm, vm, vm),
        scratch_shapes=[
            pltpu.VMEM((rows, cols), jnp.int32),
            pltpu.VMEM((2, rows, cols), jnp.int32),
            pltpu.SMEM(class_resistance.shape, F32),
            pltpu.VMEM((1, pairs), jnp.int32),
            pltpu.VMEM((1, pairs), jnp.int32),
            pltpu.VMEM((pairs * rows, cols), F32),
            pltpu.SemaphoreType.DMA((6,)),
            pltpu.VMEM((rows + 2, pairs, cols), F32),
            pltpu.VMEM((rows + 2, pairs, cols), F32),
            pltpu.VMEM((rows + 2, pairs, cols), F32),
            pltpu.VMEM((3, pairs, cols), F32),
            pltpu.VMEM((3, pairs, cols), F32),
            pltpu.VMEM((3, pairs, cols), F32),
            pltpu.VMEM((8, cols), F32),
            pltpu.VMEM((8, cols), F32),
            pltpu.VMEM((8, cols), F32),
            pltpu.VMEM((2, rows, cols), F32),
            pltpu.VMEM((2, rows, cols), F32),
            pltpu.VMEM((2, rows, cols), F32),
            pltpu.VMEM((6, rows, cols), F32),
            pltpu.VMEM((2, pairs, cols), F32),
            pltpu.SemaphoreType.DMA((3, 4)),
            pltpu.SemaphoreType.DMA((3, 4)),
            pltpu.SemaphoreType.DMA((4,)),
            pltpu.SemaphoreType.DMA((4,)),
            pltpu.SemaphoreType.DMA((nst, 3, 2)),
            pltpu.SemaphoreType.DMA((nst, 3, 2)),
            *sums, *slots,
        ],
        compiler_params=pltpu.CompilerParams(
            collective_id=0, has_side_effects=True, vmem_limit_bytes=40 * 2**20),
        name="krylov",
    )(land_cover, prune_mask, class_resistance, source_cells, ground_cells, x2d)
    full = jax.ShapeDtypeStruct(warm_start.shape, F32)
    tile = 8
    return pl.pallas_call(
        finish_kernel,
        out_shape=(full, full),
        in_specs=[vm, vm, vm, hbm],
        out_specs=(hbm, hbm),
        scratch_shapes=[
            pltpu.VMEM((pairs * rows, cols), F32),
            pltpu.VMEM((rows // tile, pairs, tile, cols), F32),
            pltpu.VMEM((rows // tile, pairs, tile, cols), F32),
            pltpu.VMEM((2 * pairs, 3 * pairs), jnp.bfloat16),
            pltpu.VMEM((2 * pairs, 3 * pairs), jnp.bfloat16),
            pltpu.SemaphoreType.DMA,
            pltpu.SemaphoreType.DMA((2, rows // tile)),
        ],
        compiler_params=pltpu.CompilerParams(vmem_limit_bytes=40 * 2**20),
        name="finish",
    )(gram, vh, vl, x2d)


def solution(mesh):
    in_specs = (
        P(("groups", "wide"), ("narrow", "inner")),
        P(None, ("groups", "wide"), ("narrow", "inner")),
        P(),
        P("groups"),
        P("groups"),
        P(None, ("groups", "wide"), ("narrow", "inner")),
    )
    out_specs = (
        P(None, ("groups", "wide"), ("narrow", "inner")),
        P(None, ("groups", "wide"), ("narrow", "inner")),
    )
    sizes = tuple(mesh.shape[a] for a in ("wide", "narrow", "inner"))
    return jax.shard_map(
        functools.partial(per_device, sizes), mesh=mesh, in_specs=in_specs, out_specs=out_specs, check_vma=False
    )
```

```python
import functools
import jax
import jax.numpy as jnp
from jax import lax
from jax.experimental import pallas as pl
from jax.experimental.pallas import tpu as pltpu
from jax.sharding import PartitionSpec as P

LEAK = 0.1
MESH = pl.DeviceIdType.MESH
F32 = jnp.float32
GROUP = 16
BLOCK = 16
STEP = 4
NT = (((1,), (1,)), ((), ()))
NN = (((1,), (0,)), ((), ()))


def split(x):
    hi = x.astype(jnp.bfloat16)
    return hi, (x - hi.astype(F32)).astype(jnp.bfloat16)


def dot3(a, b, dims):
    (ah, al), (bh, bl) = a, b
    mm = functools.partial(lax.dot_general, dimension_numbers=dims, preferred_element_type=F32)
    return mm(ah, bh) + (mm(ah, bl) + mm(al, bh))


def stages_of(count):
    out, stride = [], 1
    while count > 1:
        g = min(GROUP, count)
        assert count % g == 0
        out.append((g, stride))
        stride *= g
        count //= g
    return out


def krylov_kernel(sizes, pieces, cover_hbm, prune_hbm, table_hbm, src_hbm, gnd_hbm, x_hbm,
                  vh, vl, gram_ref,
                  cover_ref, prune_ref, table_ref, src_ref, gnd_ref, x_ref, insem, fx, f0, f1, packs, lefts, rights, edge, edge_up, edge_down, side, side_left, side_right,
                  cond, sg, hsend, hrecv, isend, irecv, gsend, grecv, *bufs):
    wide_n, narrow_n, inner_n = sizes
    pairs = fx.shape[1]
    rows, cols = cover_ref.shape
    cells_n = narrow_n * inner_n
    stages = stages_of(wide_n * cells_n)
    w = lax.axis_index("wide")
    c = lax.axis_index("narrow") * inner_n + lax.axis_index("inner")
    rank = w * cells_n + c

    def dev(rk):
        return {"wide": rk // cells_n, "narrow": (rk % cells_n) // inner_n, "inner": rk % inner_n}

    has_up, has_down = w > 0, w < wide_n - 1
    has_left, has_right = c > 0, c < cells_n - 1
    sides = ((has_up, rank - cells_n), (has_down, rank + cells_n), (has_left, rank - 1), (has_right, rank + 1))

    def peer(stage, o):
        g, stride = stages[stage]
        digit = (rank // stride) % g
        other = (digit + o) % g
        return other, rank + (other - digit) * stride

    loads = [pltpu.make_async_copy(a, b, insem.at[i]) for i, (a, b) in enumerate((
        (x_hbm, x_ref), (cover_hbm, cover_ref), (prune_hbm, prune_ref), (table_hbm, table_ref),
        (src_hbm, src_ref), (gnd_hbm, gnd_ref)))]
    for cp in loads:
        cp.start()
    barrier = pltpu.get_barrier_semaphore()
    expect = 0
    for s, (g, _) in enumerate(stages):
        for o in range(1, g):
            pl.semaphore_signal(barrier, inc=1, device_id=dev(peer(s, o)[1]), device_id_type=MESH)
            expect += 1
    near = 0
    if len(stages) > 1:
        for has, rk in sides:
            near = near + has.astype(jnp.int32)

            @pl.when(has)
            def _(rk=rk):
                pl.semaphore_signal(barrier, inc=1, device_id=dev(rk), device_id_type=MESH)

    lane = lax.broadcasted_iota(jnp.int32, (pairs, cols), 1)
    half = pairs // 2

    for cp in loads[1:4]:
        cp.wait()
    cover = cover_ref[...]
    res = jnp.zeros((rows, cols), F32)
    for k in range(table_ref.shape[0]):
        res = jnp.where(cover == k, table_ref[k], res)
    keep_r = (1 - prune_ref[0]).astype(F32)
    keep_d = (1 - prune_ref[1]).astype(F32)
    side[0] = res
    side[1] = keep_r
    edge[...] = jnp.concatenate([res[:1], res[rows - 1:], keep_d[rows - 1:], res[: 5]], 0)

    zero_row = jnp.zeros((pairs, cols), F32)
    for has, bufs0 in ((has_up, tuple(f.at[0] for f in (fx, f0, f1))),
                       (has_down, tuple(f.at[rows + 1] for f in (fx, f0, f1))),
                       (has_left, tuple(lefts.at[e] for e in range(3))),
                       (has_right, tuple(rights.at[e] for e in range(3)))):
        @pl.when(jnp.logical_not(has))
        def _(bufs0=bufs0):
            for b in bufs0:
                b[...] = zero_row

    for has, ref in ((has_up, edge_up), (has_down, edge_down), (has_left, side_left), (has_right, side_right)):
        @pl.when(jnp.logical_not(has))
        def _(ref=ref):
            ref[...] = jnp.ones(ref.shape, F32)

    packs[0] = zero_row
    lane_r = lax.broadcasted_iota(jnp.int32, (rows, cols), 1)
    row_r = lax.broadcasted_iota(jnp.int32, (rows, cols), 0)
    cond[5] = ((lane_r == 2 * row_r) | (lane_r == (2 * row_r + cols - 1) % cols)).astype(F32)
    loads[0].wait()

    def load_rows(i, carry):
        pack = packs[0]
        for d in range(STEP):
            r = i * STEP + d
            v = x_ref[pl.ds(r, pairs, stride=rows), :]
            fx[r + 1] = v
            pack = pack + pltpu.roll(v, 2 * r, 1) * cond[5, pl.ds(r, 1), :]
        packs[0] = pack
        return carry

    last_step = rows // STEP - 1
    lax.fori_loop(0, 2, lambda i, carry: load_rows(i * last_step, carry), 0)
    pl.semaphore_wait(barrier, expect + near)

    def halo(e):
        field = (fx, f0, f1)[e]
        return (
            (field.at[1], field.at[rows + 1], 0),
            (field.at[rows], field.at[0], 1),
            (packs.at[e], rights.at[e], 2),
            (packs.at[e], lefts.at[e], 3),
        )

    def copies(items, ssem, rsem):
        out = []
        for (src, dst, k), (has, rk) in zip(items, sides):
            out.append((has, pltpu.make_async_remote_copy(
                src_ref=src, dst_ref=dst, send_sem=ssem.at[k], recv_sem=rsem.at[k],
                device_id=dev(rk), device_id_type=MESH)))
        return out

    def start(cs):
        for has, cp in cs:
            @pl.when(has)
            def _(cp=cp):
                cp.start()

    def wait(cs):
        order = (1, 0, 3, 2)
        for k, (has, cp) in enumerate(cs):
            @pl.when(has)
            def _(cp=cp):
                cp.wait_send()

            @pl.when(cs[order[k]][0])
            def _(cp=cp):
                cp.wait_recv()

    info = copies(((edge, edge_down, 0), (edge, edge_up, 1), (side, side_right, 2), (side, side_left, 3)), isend, irecv)
    start(info)
    ex = [copies(halo(e), hsend.at[e], hrecv.at[e]) for e in range(3)]
    start(ex[0][:2])
    lax.fori_loop(1, last_step, load_rows, 0)
    start(ex[0][2:])

    for cp in loads[4:]:
        cp.wait()
    src_t = jnp.broadcast_to(src_ref[...].astype(F32), (cols, pairs)).T
    gnd_t = jnp.broadcast_to(gnd_ref[...].astype(F32), (cols, pairs)).T
    sg[0] = src_t
    sg[1] = gnd_t

    wait(info)
    right_res = jnp.where(lane_r == cols - 1, pltpu.roll(side_right[0], cols - 1, 1), pltpu.roll(res, cols - 1, 1))
    left_res = jnp.where(lane_r == 0, pltpu.roll(side_left[0], 1, 1), pltpu.roll(res, 1, 1))
    left_keep = jnp.where(lane_r == 0, pltpu.roll(side_left[1], 1, 1), pltpu.roll(keep_r, 1, 1))
    down_res = jnp.where(row_r == rows - 1, edge_down[0:1, :], pltpu.roll(res, rows - 1, 0))
    up_res = jnp.where(row_r == 0, edge_up[1:2, :], pltpu.roll(res, 1, 0))
    up_keep = jnp.where(row_r == 0, edge_up[2:3, :], pltpu.roll(keep_d, 1, 0))
    at_right = (lane_r == cols - 1) & jnp.logical_not(has_right)
    at_left = (lane_r == 0) & jnp.logical_not(has_left)
    at_down = (row_r == rows - 1) & jnp.logical_not(has_down)
    at_up = (row_r == 0) & jnp.logical_not(has_up)
    to_right = jnp.where(at_right, 0.0, keep_r * 2.0 / (res + right_res))
    to_left = jnp.where(at_left, 0.0, left_keep * 2.0 / (res + left_res))
    cond[0] = jnp.where(lane_r == cols - 1, 0.0, to_right)
    cond[1] = jnp.where(lane_r == 0, 0.0, to_left)
    cond[4] = jnp.where(lane_r == cols - 1, to_right, jnp.where(lane_r == 0, to_left, 0.0))
    cond[2] = jnp.where(at_down, 0.0, keep_d * 2.0 / (res + down_res))
    cond[3] = jnp.where(at_up, 0.0, up_keep * 2.0 / (res + up_res))

    def stencil(e, finish):
        field = (fx, f0, f1)[e]
        even = (lane % 2) == 0
        lefts[e] = jnp.where(even, rights[e], pltpu.roll(lefts[e], 2, 1))
        if e < 2:
            packs[e + 1] = zero_row

        def body(i, carry):
            for h in range(2):
                hs = pl.ds(h * half, half)
                halos = lefts[e, hs, :]
                pack = packs[e + 1, hs, :] if e < 2 else None
                for d in range(STEP):
                    r = i * STEP + d
                    cr, cl, cd, cu, ce, pm = (cond[k, pl.ds(r, 1), :] for k in range(6))
                    v = field[r + 1, hs, :]
                    edges = pltpu.roll(halos, (2 * cols - 2 * r - 1) % cols, 1)
                    xr = pltpu.roll(v, cols - 1, 1)
                    xl = pltpu.roll(v, 1, 1)
                    lap = cr * (v - xr) + cl * (v - xl) + ce * (v - edges) + cd * (v - field[r + 2, hs, :]) + cu * (v - field[r, hs, :])
                    out = finish(r, hs, v, lap)
                    if e < 2:
                        (f0, f1)[e][r + 1, hs, :] = out
                        pack = pack + pltpu.roll(out, 2 * r, 1) * pm
                    at = (pl.ds(e * pairs + h * half, half), pl.ds(pl.multiple_of(r * cols, cols), cols))
                    hi, lo = split(out)
                    vh[at] = hi
                    vl[at] = lo
                if e < 2:
                    packs[e + 1, hs, :] = pack
            return carry

        last = rows // STEP - 1
        lax.fori_loop(0, 2, lambda i, carry: body(i * last, carry), 0)
        if e < 2:
            start(ex[e + 1][:2])
        lax.fori_loop(1, last, body, 0)
        if e < 2:
            start(ex[e + 1][2:])

    total_cols = cols * cells_n
    col_f = (lax.broadcasted_iota(jnp.int32, (1, cols), 1) + c * cols)

    def first(r, hs, v, lap):
        flat = (col_f + (w * rows + r) * total_cols).astype(F32)
        cur = (sg[0, hs, :] == flat).astype(F32) - (sg[1, hs, :] == flat).astype(F32)
        out = cur - (LEAK * v + lap)
        return out

    def second(r, hs, v, lap):
        return lap

    def part(lo, hi):
        return vh[lo * pairs:hi * pairs, :], vl[lo * pairs:hi * pairs, :]

    nst = len(stages)
    gl = bufs[:nst + 1]
    rb = bufs[nst + 1:]
    offs = [sum(pieces[:k]) for k in range(len(pieces))]

    def reduce_start(s, k):
        g, _ = stages[s]
        n = pieces[k] // g
        for o in range(1, g):
            other, rk = peer(s, o)
            pltpu.make_async_remote_copy(
                src_ref=gl[s].at[pl.ds(pl.multiple_of(offs[k] + other * n, 8), n)],
                dst_ref=rb[s * len(pieces) + k].at[o - 1],
                send_sem=gsend.at[s, k, 0], recv_sem=grecv.at[s, k, 0],
                device_id=dev(rk), device_id_type=MESH).start()

    def wait_all(s, k, phase):
        buf = rb[s * len(pieces) + k]
        pltpu.make_async_copy(buf, buf, gsend.at[s, k, phase]).wait()
        pltpu.make_async_copy(buf, buf, grecv.at[s, k, phase]).wait()

    def reduce_finish(s, k):
        g, stride = stages[s]
        n = pieces[k] // g
        wait_all(s, k, 0)
        me = (rank // stride) % g
        mine = pl.ds(pl.multiple_of(offs[k] + me * n, 8), n)
        total = gl[s][mine, :]
        for o in range(g - 1):
            total = total + rb[s * len(pieces) + k][o]
        gl[s + 1][mine, :] = total
        for o in range(1, g):
            _, rk = peer(s, o)
            pltpu.make_async_remote_copy(
                src_ref=gl[s + 1].at[mine], dst_ref=gl[s + 1].at[mine],
                send_sem=gsend.at[s, k, 1], recv_sem=grecv.at[s, k, 1],
                device_id=dev(rk), device_id_type=MESH).start()

    wait(ex[0])
    stencil(0, first)

    gl[0][0:pairs, :] = dot3(part(0, 1), part(0, 1), NT)
    reduce_start(0, 0)
    wait(ex[1])
    stencil(1, second)

    reduce_finish(0, 0)
    gl[0][pairs:3 * pairs, :] = dot3(part(0, 2), part(1, 2), NT)
    reduce_start(0, 1)
    wait(ex[2])
    stencil(2, second)

    reduce_finish(0, 1)
    gl[0][3 * pairs:, :] = dot3(part(1, 2), part(2, 3), NT)
    reduce_start(0, 2)
    reduce_finish(0, 2)
    for k in range(3):
        wait_all(0, k, 1)
    for s in range(1, nst):
        for k in range(3):
            reduce_start(s, k)
        for k in range(3):
            reduce_finish(s, k)
        for k in range(3):
            wait_all(s, k, 1)
    gram_ref[...] = gl[nst][...]


def mm(a, b):
    return lax.dot_general(a, b, NN, precision=lax.Precision.HIGHEST, preferred_element_type=F32)


def split3(x):
    h1 = x.astype(jnp.bfloat16)
    rest = x - h1.astype(F32)
    h2 = rest.astype(jnp.bfloat16)
    return h1, h2, (rest - h2.astype(F32)).astype(jnp.bfloat16)


def eliminate(systems):
    n = systems[0][0].shape[0]
    state = [list(s) for s in systems]
    lane = lax.broadcasted_iota(jnp.int32, (n, n), 1)
    row = lax.broadcasted_iota(jnp.int32, (n, n), 0)
    sub = lax.broadcasted_iota(jnp.int32, (BLOCK, n), 0)
    slot = lane // BLOCK
    second, third = (slot == 2) | (slot == 5), slot == 4
    assert n == 8 * BLOCK
    for k in range(n // BLOCK):
        lo, hi = k * BLOCK, (k + 1) * BLOCK
        inside = (row >= lo) & (row < hi)
        lhs_mask = (lane >= lo) & (lane < hi) & jnp.logical_not(inside)
        panels, lefts = [], []
        for mats in state:
            t = jnp.where(lhs_mask, mats[0], 0.0)
            for shift in (BLOCK, 2 * BLOCK, 4 * BLOCK):
                t = t + pltpu.roll(t, shift, 1)
            h1 = t.astype(jnp.bfloat16).astype(F32)
            h2 = (t - h1).astype(jnp.bfloat16).astype(F32)
            h3 = t - h1 - h2
            lefts.append(jnp.where(third, h3, jnp.where(second, h2, h1)).astype(jnp.bfloat16))
            pan = [m[lo:hi, :] for m in mats]
            panels.append(([jnp.broadcast_to(pan[0][:, lo + j:lo + j + 1], (BLOCK, n)) for j in range(BLOCK)], pan))
        for i in range(BLOCK):
            for cs, pan in panels:
                f = cs[i]
                rinv = pl.reciprocal(f[i:i + 1, :])

                def step(t):
                    top = t[i:i + 1, :]
                    prod = f * top
                    return jnp.where(sub == i, top * rinv, t - prod * rinv)

                for j in range(i + 1, BLOCK):
                    cs[j] = step(cs[j])
                for q in range(len(pan)):
                    pan[q] = step(pan[q])
        for mats, lhs, (_, pan) in zip(state, lefts, panels):
            q1, q2, q3 = split3(jnp.concatenate(pan, 1))
            none = jnp.zeros((n - 6 * BLOCK, q1.shape[1]), jnp.bfloat16)
            rhs = jnp.concatenate([q1, q2, q1, q3, q1, q2, none], 0)
            change = lax.dot_general(lhs, rhs, NN, preferred_element_type=F32)
            for q in range(len(mats)):
                parts = [pan[q]]
                if lo:
                    parts.insert(0, mats[q][:lo] - change[:lo, q * n:(q + 1) * n])
                if hi < n:
                    parts.append(mats[q][hi:] - change[hi:, q * n:(q + 1) * n])
                mats[q] = jnp.concatenate(parts, 0)
    return [s[1:] for s in state]


def finish_kernel(gram_ref, vh, vl, x_hbm, out_x, out_r, x_ref, bx, br, ch, cl, insem, outsem):
    groups, n, tile, cols = bx.shape
    rows = groups * tile
    load = pltpu.make_async_copy(x_hbm, x_ref, insem)
    load.start()

    def sym(m):
        return 0.5 * (m + m.T)

    g = sym(gram_ref[0:n, :])
    e = sym(gram_ref[n:2 * n, :])
    f = sym(gram_ref[2 * n:3 * n, :])
    h = sym(gram_ref[3 * n:, :])
    eye = (lax.broadcasted_iota(jnp.int32, (n, n), 0) == lax.broadcasted_iota(jnp.int32, (n, n), 1)).astype(F32)
    (a, ap), (ginv,) = eliminate([(LEAK * g + e, g, e), (g, eye)])
    rr = sym(mm(a.T, mm(f, a) - mm(e, ap)))
    p = ap + mm(ginv, rr)
    curv = sym(mm(a.T, mm(LEAK * f + h, a) - mm(LEAK * e + f, p)))
    ((al,),) = eliminate([(curv, rr)])
    q = mm(a, al)
    pq = mm(p, al)
    zero = jnp.zeros((n, n), F32)
    top = jnp.concatenate([(a + pq).T, -q.T, zero], 1)
    bottom = jnp.concatenate([(ap - LEAK * pq).T, (LEAK * q - a - pq).T, q.T], 1)
    hi, lo = split(jnp.concatenate([top, bottom], 0))
    ch[...] = hi
    cl[...] = lo

    load.wait()
    stores = []
    for g in range(groups):
        for i in range(tile // 2):
            at = pl.ds((g * tile + 2 * i) * cols, 2 * cols)
            out = dot3((ch[...], cl[...]), (vh[:, at], vl[:, at]), NN)
            for d in range(2):
                r = 2 * i + d
                here = pl.ds(r, n, stride=tile)
                bx.at[g].reshape(n * tile, cols)[here, :] = (
                    x_ref[pl.ds(g * tile + r, n, stride=rows), :] + out[:n, d * cols:(d + 1) * cols])
                br.at[g].reshape(n * tile, cols)[here, :] = out[n:, d * cols:(d + 1) * cols]
        for j, (buf, dst) in enumerate(((bx, out_x), (br, out_r))):
            cp = pltpu.make_async_copy(buf.at[g], dst.at[:, pl.ds(g * tile, tile), :], outsem.at[j, g])
            cp.start()
            stores.append(cp)
    for cp in stores:
        cp.wait()


def per_device(sizes, land_cover, prune_mask, class_resistance, source_cells, ground_cells, warm_start):
    rows, cols = land_cover.shape
    pairs = warm_start.shape[0]
    pieces = (pairs, 2 * pairs, pairs)
    count = sizes[0] * sizes[1] * sizes[2]
    stages = stages_of(count)
    nst = max(1, len(stages))
    x2d, land_cover, prune_mask, class_resistance, source_cells, ground_cells = (
        pltpu.with_memory_space_constraint(v, pltpu.HBM) for v in (
            warm_start.reshape(pairs * rows, cols), land_cover, prune_mask, class_resistance,
            source_cells.reshape(1, pairs), ground_cells.reshape(1, pairs)))
    basis = jax.ShapeDtypeStruct((3 * pairs, rows * cols), jnp.bfloat16)
    hbm = pl.BlockSpec(memory_space=pltpu.HBM)
    vm = pl.BlockSpec(memory_space=pltpu.VMEM)
    sums = [pltpu.VMEM((4 * pairs, pairs), F32) for _ in range(nst + 1)]
    slots = [pltpu.VMEM((g - 1, n // g, pairs), F32) for g, _ in stages for n in pieces]
    vh, vl, gram = pl.pallas_call(
        functools.partial(krylov_kernel, sizes, pieces),
        out_shape=(basis, basis, jax.ShapeDtypeStruct((4 * pairs, pairs), F32)),
        in_specs=[hbm] * 6,
        out_specs=(vm, vm, vm),
        scratch_shapes=[
            pltpu.VMEM((rows, cols), jnp.int32),
            pltpu.VMEM((2, rows, cols), jnp.int32),
            pltpu.SMEM(class_resistance.shape, F32),
            pltpu.VMEM((1, pairs), jnp.int32),
            pltpu.VMEM((1, pairs), jnp.int32),
            pltpu.VMEM((pairs * rows, cols), F32),
            pltpu.SemaphoreType.DMA((6,)),
            pltpu.VMEM((rows + 2, pairs, cols), F32),
            pltpu.VMEM((rows + 2, pairs, cols), F32),
            pltpu.VMEM((rows + 2, pairs, cols), F32),
            pltpu.VMEM((3, pairs, cols), F32),
            pltpu.VMEM((3, pairs, cols), F32),
            pltpu.VMEM((3, pairs, cols), F32),
            pltpu.VMEM((8, cols), F32),
            pltpu.VMEM((8, cols), F32),
            pltpu.VMEM((8, cols), F32),
            pltpu.VMEM((2, rows, cols), F32),
            pltpu.VMEM((2, rows, cols), F32),
            pltpu.VMEM((2, rows, cols), F32),
            pltpu.VMEM((6, rows, cols), F32),
            pltpu.VMEM((2, pairs, cols), F32),
            pltpu.SemaphoreType.DMA((3, 4)),
            pltpu.SemaphoreType.DMA((3, 4)),
            pltpu.SemaphoreType.DMA((4,)),
            pltpu.SemaphoreType.DMA((4,)),
            pltpu.SemaphoreType.DMA((nst, 3, 2)),
            pltpu.SemaphoreType.DMA((nst, 3, 2)),
            *sums, *slots,
        ],
        compiler_params=pltpu.CompilerParams(
            collective_id=0, has_side_effects=True, vmem_limit_bytes=40 * 2**20),
        name="krylov",
    )(land_cover, prune_mask, class_resistance, source_cells, ground_cells, x2d)
    full = jax.ShapeDtypeStruct(warm_start.shape, F32)
    tile = 8
    return pl.pallas_call(
        finish_kernel,
        out_shape=(full, full),
        in_specs=[vm, vm, vm, hbm],
        out_specs=(hbm, hbm),
        scratch_shapes=[
            pltpu.VMEM((pairs * rows, cols), F32),
            pltpu.VMEM((rows // tile, pairs, tile, cols), F32),
            pltpu.VMEM((rows // tile, pairs, tile, cols), F32),
            pltpu.VMEM((2 * pairs, 3 * pairs), jnp.bfloat16),
            pltpu.VMEM((2 * pairs, 3 * pairs), jnp.bfloat16),
            pltpu.SemaphoreType.DMA,
            pltpu.SemaphoreType.DMA((2, rows // tile)),
        ],
        compiler_params=pltpu.CompilerParams(vmem_limit_bytes=40 * 2**20),
        name="finish",
    )(gram, vh, vl, x2d)


def solution(mesh):
    in_specs = (
        P(("groups", "wide"), ("narrow", "inner")),
        P(None, ("groups", "wide"), ("narrow", "inner")),
        P(),
        P("groups"),
        P("groups"),
        P(None, ("groups", "wide"), ("narrow", "inner")),
    )
    out_specs = (
        P(None, ("groups", "wide"), ("narrow", "inner")),
        P(None, ("groups", "wide"), ("narrow", "inner")),
    )
    sizes = tuple(mesh.shape[a] for a in ("wide", "narrow", "inner"))
    return jax.shard_map(
        functools.partial(per_device, sizes), mesh=mesh, in_specs=in_specs, out_specs=out_specs, check_vma=False
    )
```
